256 devices in a mesh: col: 128 (over y_lo, x, z, core), orb: 2 (over y_hi).
Axes of the slice: x: 4, y: 4 (y_hi: 2, y_lo: 2; y = y_hi * 2 + y_lo), z: 8, core: 2. Of those that a mesh axis runs over, the one named last changes fastest.
Arguments:
- slab_occ: bfloat16 [1024, 400], P('col', 'orb'), may hold values from -6 to 6
- slab_vir: bfloat16 [1024, 2400], P('col', 'orb'), may hold values from -6 to 6
- orbitals_occ: bfloat16 [400, 131072], P('orb', 'col'), may hold values from -0.3125 to 0.3125
- orbitals_vir: bfloat16 [2400, 131072], P('orb', 'col'), may hold values from -0.125 to 0.125
- occ_energy: float32 [400], P('orb'), may hold values from -2 to -0.1
- vir_energy: float32 [2400], P('orb'), may hold values from 0.1 to 3
- screened: bfloat16 [1024, 131072], P('col'), may hold values from -6 to 6
Outputs:
- occ_kernel: bfloat16 [1024, 400], P(('col', 'orb'))
- vir_kernel: bfloat16 [1024, 2400], P(('col', 'orb'))
The draws below stay inside these ranges and needn't reach their ends.
All inputs are finite; a program needn't handle non-finite values.
Results may differ from the reference program's by a relative error of at most 0.014.
Values may be sent and summed in bfloat16 or wider, within the bound.
No kernel may reach another device: no remote copies, remote signals or barrier semaphores. Data moves between devices by JAX's collectives and lax.ppermute only.
A program may use at most 64 MiB of HBM per device.

```python
import jax
import jax.numpy as jnp
from jax import lax

NO = 400
NV = 2400
ROWS = 1024
COL_DEV = 1024
NR = 131072


def with_spikes(result, own_key, source, target, parts, factor):
    owner, partner = [(jnp.arange(result.shape[position]) // (result.shape[position] // parts)).reshape([-1 if axis == position else 1 for axis in range(result.ndim)]) for position in (source, target)]
    chosen = jax.random.permutation(own_key, parts)[partner]
    strong = (owner == chosen) | (owner == (partner + parts // 2) % parts)
    return jnp.where(strong, factor * result, result)


def levels(key, shape, split, smallest, high):
    level, own = 1.0, jax.random.fold_in(key, 6)
    for position, blocks in split:
        heights = jnp.exp(jax.random.uniform(jax.random.fold_in(own, position), (blocks,), jnp.float32, smallest / len(split), high / len(split)))
        level = level * jnp.repeat(heights, shape[position] // blocks).reshape([-1 if axis == position else 1 for axis in range(len(shape))])
    return level


def gaussian(key, extent, deviation, most, split=(), kind=jnp.bfloat16):
    entries = jax.random.normal(key, extent, jnp.float32) * deviation
    if len(split) > 0:
        entries = levels(key, extent, split, -0.22, 0.18) * entries
    return jnp.clip(entries, min=-most, max=most).astype(kind)


def bell_draw_with(rng, extent, scale, reach, split, heavy, kind=jnp.bfloat16):
    result = scale * jax.random.normal(rng, extent, jnp.float32)
    if split:
        result = result * levels(rng, extent, split, -0.22, 0.18)
    return jnp.clip(with_spikes(result, jax.random.fold_in(rng, 3), *heavy), -reach, reach).astype(kind)


def setup_inputs(seed: int = 0) -> dict:
    keys = jax.random.split(jax.random.key(seed), 8)
    return {
        "slab_occ": gaussian(keys[0], (ROWS, NO), 1.0, 6.0, ((0, 128), (1, 2))),
        "slab_vir": gaussian(keys[1], (ROWS, NV), 1.0, 6.0, ((0, 128), (1, 2))),
        "orbitals_occ": gaussian(keys[2], (NO, NR), NO ** -0.5, 0.3125, ((0, 2), (1, 128))),
        "orbitals_vir": gaussian(keys[3], (NV, NR), NV ** -0.5, 0.125, ((0, 2), (1, 128))),
        "occ_energy": jnp.clip(-2.0 + 1.9 * jax.random.uniform(keys[4], (NO,), jnp.float32) ** levels(keys[4], (NO,), ((0, 2),), -0.2, 0.2), -2.0, -0.1),
        "vir_energy": jnp.clip(0.1 + 2.9 * jax.random.uniform(keys[5], (NV,), jnp.float32) ** levels(keys[5], (NV,), ((0, 2),), -0.2, 0.2), 0.1, 3.0),
        "screened": bell_draw_with(keys[6], (ROWS, NR), (80 / NR ** 0.5), 6.0, ((0, 128),), (1, 0, 128, 5.5)),
    }


def reference(slab_occ, slab_vir, orbitals_occ, orbitals_vir, occ_energy, vir_energy, screened):
    scaled_occ = (slab_occ.astype(jnp.float32) * jnp.exp(occ_energy)[None, :]).astype(jnp.bfloat16)
    scaled_vir = (slab_vir.astype(jnp.float32) * jnp.exp(-vir_energy)[None, :]).astype(jnp.bfloat16)
    width = COL_DEV
    count = NR // width

    def advance(carry, index):
        acc_occ, acc_vir = carry
        start = (index * width).astype(jnp.int32)
        occ_cols = lax.dynamic_slice_in_dim(orbitals_occ, start, width, 1)
        vir_cols = lax.dynamic_slice_in_dim(orbitals_vir, start, width, 1)
        screen = lax.dynamic_slice_in_dim(screened, start, width, 1).astype(jnp.float32)
        green_occ = jnp.dot(scaled_occ, occ_cols, preferred_element_type=jnp.float32)
        green_vir = jnp.dot(scaled_vir, vir_cols, preferred_element_type=jnp.float32)
        occ_side = (green_vir * screen).astype(jnp.bfloat16)
        vir_side = (green_occ * screen).astype(jnp.bfloat16)
        dims = (((1,), (1,)), ((), ()))
        acc_occ = acc_occ + lax.dot_general(occ_side, occ_cols, dims, preferred_element_type=jnp.float32)
        acc_vir = acc_vir + lax.dot_general(vir_side, vir_cols, dims, preferred_element_type=jnp.float32)
        return (acc_occ, acc_vir), None

    init = (jnp.zeros((ROWS, NO), jnp.float32), jnp.zeros((ROWS, NV), jnp.float32))
    (acc_occ, acc_vir), unused = lax.scan(advance, init, jnp.arange(count, dtype=jnp.int32))
    return acc_occ.astype(jnp.bfloat16), acc_vir.astype(jnp.bfloat16)
```

```python
import jax
import jax.numpy as jnp
from jax import lax
from jax.sharding import Mesh, PartitionSpec as P

SWAP = ((0, 1), (1, 0))
CHIPS = ("yl", "x", "z")


def spread(block, axes):
    count = lax.axis_size(axes)
    copies = jnp.broadcast_to(block[None], (count,) + block.shape)
    arrived = lax.all_to_all(copies, axes, 0, 0, tiled=True)
    return arrived.reshape((count * block.shape[0],) + block.shape[1:])


def both_cores(own, core):
    other = lax.ppermute(own, "core", SWAP)
    first = jnp.where(core == 0, own, other)
    second = jnp.where(core == 0, other, own)
    return jnp.concatenate([first, second], axis=1)


def local(slab_occ, slab_vir, orbitals_occ, orbitals_vir, occ_energy, vir_energy, screened):
    f32, bf16 = jnp.float32, jnp.bfloat16
    core, part = lax.axis_index("core"), lax.axis_index("orb")
    half = orbitals_occ.shape[1]
    n_occ, n_vir = orbitals_occ.shape[0], orbitals_vir.shape[0]

    screen = lax.all_to_all(screened, CHIPS, split_axis=1, concat_axis=0, tiled=True)

    scaled_occ = (slab_occ.astype(f32) * jnp.exp(occ_energy)[None, :]).astype(bf16)
    scaled_vir = (slab_vir.astype(f32) * jnp.exp(-vir_energy)[None, :]).astype(bf16)
    scaled = jnp.concatenate(
        [scaled_vir, scaled_occ, lax.ppermute(scaled_occ, "orb", SWAP)], axis=1
    )
    slab = spread(spread(scaled, "z"), ("yl", "x"))
    near_vir, near_occ = slab[:, :n_vir], slab[:, n_vir:]

    vir = both_cores(orbitals_vir, core)
    all_occ = jnp.concatenate([orbitals_occ, lax.ppermute(orbitals_occ, "orb", SWAP)], axis=0)
    occ = both_cores(all_occ, core)

    send_vir = lax.dynamic_slice_in_dim(vir, (1 - part) * half, half, 1)
    keep_vir = lax.dynamic_slice_in_dim(vir, part * half, half, 1)
    away = jnp.dot(near_vir, send_vir, preferred_element_type=f32).astype(bf16)
    arrived = lax.ppermute(away, "orb", SWAP)
    green_vir = jnp.dot(near_vir, keep_vir, preferred_element_type=f32) + arrived.astype(f32)
    keep_screen = lax.dynamic_slice_in_dim(screen, part * half, half, 1)
    keep_occ = lax.dynamic_slice_in_dim(occ, part * half, half, 1)
    occ_side = (green_vir * keep_screen.astype(f32)).astype(bf16)

    green_occ = jnp.dot(near_occ, occ, preferred_element_type=f32)
    vir_side = (green_occ * screen.astype(f32)).astype(bf16)

    dims = (((1,), (1,)), ((), ()))
    occ_term = lax.dot_general(occ_side, keep_occ, dims, preferred_element_type=f32)
    vir_term = lax.dot_general(vir_side, vir, dims, preferred_element_type=f32)
    terms = jnp.concatenate([vir_term.astype(bf16), occ_term.astype(bf16)], axis=1)

    axes = CHIPS + ("orb",)
    owners = lax.axis_size(axes)
    rows = terms.shape[0] // owners
    terms = terms.reshape((owners, rows, terms.shape[1]))
    terms = lax.all_to_all(terms, axes, 0, 0, tiled=True)
    terms = terms.reshape((owners // 2, 2, rows, terms.shape[2])).astype(f32)
    total = jnp.sum(terms, axis=0)
    vir_total = jnp.concatenate([total[0, :, :n_vir], total[1, :, :n_vir]], axis=1)
    occ_first, occ_second = total[0, :, n_vir:], total[1, :, n_vir:]
    occ_total = occ_first + jnp.concatenate(
        [occ_second[:, n_occ:], occ_second[:, :n_occ]], axis=1
    )
    return occ_total.astype(bf16), vir_total.astype(bf16)


def solution(mesh):
    chips = Mesh(mesh.devices.reshape(2, 4, 8, 2, 2), ("yl", "x", "z", "core", "orb"))
    col = ("yl", "x", "z", "core")
    return jax.shard_map(
        local,
        mesh=chips,
        in_specs=(
            P(col, "orb"),
            P(col, "orb"),
            P("orb", col),
            P("orb", col),
            P("orb"),
            P("orb"),
            P(col, None),
        ),
        out_specs=(P(col + ("orb",), None), P(col + ("orb",), None)),
        check_vma=False,
    )
```

```python
import jax
import jax.numpy as jnp
from jax import lax
from jax.sharding import Mesh, PartitionSpec as P

SWAP = ((0, 1), (1, 0))
CHIPS = ("yl", "x", "z")


def collect(block, axis, dim):
    count, me = lax.axis_size(axis), lax.axis_index(axis)
    shape = block.shape[:dim] + (count,) + block.shape[dim + 1 :]
    held = lax.dynamic_update_slice_in_dim(jnp.zeros(shape, block.dtype), block, me, dim)
    for step in range(1, count):
        piece = lax.ppermute(block, axis, [(i, i ^ step) for i in range(count)])
        held = lax.dynamic_update_slice_in_dim(held, piece, me ^ step, dim)
    return held


def double(block, axis, dim):
    count, me = lax.axis_size(axis), lax.axis_index(axis)
    step = 1
    while step < count:
        piece = lax.ppermute(block, axis, [(i, i ^ step) for i in range(count)])
        low = (me & step) == 0
        block = jnp.concatenate(
            [jnp.where(low, block, piece), jnp.where(low, piece, block)], axis=dim
        )
        step *= 2
    return block


def both_cores(own, core):
    other = lax.ppermute(own, "core", SWAP)
    first = jnp.where(core == 0, own, other)
    second = jnp.where(core == 0, other, own)
    return jnp.concatenate([first, second], axis=1)


def local(slab_occ, slab_vir, orbitals_occ, orbitals_vir, occ_energy, vir_energy, screened):
    f32, bf16 = jnp.float32, jnp.bfloat16
    core, part = lax.axis_index("core"), lax.axis_index("orb")
    half = orbitals_occ.shape[1]
    n_occ, n_vir = orbitals_occ.shape[0], orbitals_vir.shape[0]

    screen = lax.all_to_all(screened, CHIPS, split_axis=1, concat_axis=0, tiled=True)

    scaled_occ = (slab_occ.astype(f32) * jnp.exp(occ_energy)[None, :]).astype(bf16)
    scaled_vir = (slab_vir.astype(f32) * jnp.exp(-vir_energy)[None, :]).astype(bf16)
    scaled = jnp.concatenate(
        [scaled_vir, scaled_occ, lax.ppermute(scaled_occ, "orb", SWAP)], axis=1
    )
    slab = collect(scaled[None, None, None], "yl", 0)
    slab = double(slab, "z", 2)
    slab = collect(slab, "x", 1)
    slab = slab.reshape((-1, scaled.shape[1]))
    near_vir, near_occ = slab[:, :n_vir], slab[:, n_vir:]

    vir = both_cores(orbitals_vir, core)
    all_occ = jnp.concatenate([orbitals_occ, lax.ppermute(orbitals_occ, "orb", SWAP)], axis=0)
    occ = both_cores(all_occ, core)

    send_vir = lax.dynamic_slice_in_dim(vir, (1 - part) * half, half, 1)
    keep_vir = lax.dynamic_slice_in_dim(vir, part * half, half, 1)
    away = jnp.dot(near_vir, send_vir, preferred_element_type=f32).astype(bf16)
    arrived = lax.ppermute(away, "orb", SWAP)
    green_vir = jnp.dot(near_vir, keep_vir, preferred_element_type=f32) + arrived.astype(f32)
    keep_screen = lax.dynamic_slice_in_dim(screen, part * half, half, 1)
    keep_occ = lax.dynamic_slice_in_dim(occ, part * half, half, 1)
    occ_side = (green_vir * keep_screen.astype(f32)).astype(bf16)

    green_occ = jnp.dot(near_occ, occ, preferred_element_type=f32)
    vir_side = (green_occ * screen.astype(f32)).astype(bf16)

    dims = (((1,), (1,)), ((), ()))
    occ_term = lax.dot_general(occ_side, keep_occ, dims, preferred_element_type=f32)
    vir_term = lax.dot_general(vir_side, vir, dims, preferred_element_type=f32)
    terms = jnp.concatenate([vir_term.astype(bf16), occ_term.astype(bf16)], axis=1)

    axes = CHIPS + ("orb",)
    owners = lax.axis_size(axes)
    rows = terms.shape[0] // owners
    terms = terms.reshape((owners, rows, terms.shape[1]))
    terms = lax.all_to_all(terms, axes, 0, 0, tiled=True)
    terms = terms.reshape((owners // 2, 2, rows, terms.shape[2])).astype(f32)
    total = jnp.sum(terms, axis=0)
    vir_total = jnp.concatenate([total[0, :, :n_vir], total[1, :, :n_vir]], axis=1)
    occ_first, occ_second = total[0, :, n_vir:], total[1, :, n_vir:]
    occ_total = occ_first + jnp.concatenate(
        [occ_second[:, n_occ:], occ_second[:, :n_occ]], axis=1
    )
    return occ_total.astype(bf16), vir_total.astype(bf16)


def solution(mesh):
    chips = Mesh(mesh.devices.reshape(2, 4, 8, 2, 2), ("yl", "x", "z", "core", "orb"))
    col = ("yl", "x", "z", "core")
    return jax.shard_map(
        local,
        mesh=chips,
        in_specs=(
            P(col, "orb"),
            P(col, "orb"),
            P("orb", col),
            P("orb", col),
            P("orb"),
            P("orb"),
            P(col, None),
        ),
        out_specs=(P(col + ("orb",), None), P(col + ("orb",), None)),
        check_vma=False,
    )
```

```python
import jax
import jax.numpy as jnp
from jax import lax
from jax.sharding import Mesh, PartitionSpec as P

SWAP = ((0, 1), (1, 0))
CHIPS = ("yl", "x", "z")


def collect(block, axis, dim):
    count, me = lax.axis_size(axis), lax.axis_index(axis)
    shape = block.shape[:dim] + (count,) + block.shape[dim + 1 :]
    held = lax.dynamic_update_slice_in_dim(jnp.zeros(shape, block.dtype), block, me, dim)
    for step in range(1, count):
        piece = lax.ppermute(block, axis, [(i, i ^ step) for i in range(count)])
        held = lax.dynamic_update_slice_in_dim(held, piece, me ^ step, dim)
    return held


def spread(block, axes):
    count = lax.axis_size(axes)
    copies = jnp.broadcast_to(block[None], (count,) + block.shape)
    arrived = lax.all_to_all(copies, axes, 0, 0, tiled=True)
    return arrived.reshape((count * block.shape[0],) + block.shape[1:])


def both_cores(own, core):
    other = lax.ppermute(own, "core", SWAP)
    first = jnp.where(core == 0, own, other)
    second = jnp.where(core == 0, other, own)
    return jnp.concatenate([first, second], axis=1)


def local(slab_occ, slab_vir, orbitals_occ, orbitals_vir, occ_energy, vir_energy, screened):
    f32, bf16 = jnp.float32, jnp.bfloat16
    core, part = lax.axis_index("core"), lax.axis_index("orb")
    half = orbitals_occ.shape[1]
    n_occ, n_vir = orbitals_occ.shape[0], orbitals_vir.shape[0]

    raw = spread(jnp.concatenate([slab_vir, slab_occ], axis=1), "z")
    raw, screened = lax.optimization_barrier((raw, screened))

    screen = lax.all_to_all(screened, CHIPS, split_axis=1, concat_axis=0, tiled=True)

    scaled_vir = (raw[:, :n_vir].astype(f32) * jnp.exp(-vir_energy)[None, :]).astype(bf16)
    scaled_occ = (raw[:, n_vir:].astype(f32) * jnp.exp(occ_energy)[None, :]).astype(bf16)
    scaled = jnp.concatenate(
        [scaled_vir, scaled_occ, lax.ppermute(scaled_occ, "orb", SWAP)], axis=1
    )
    slab = collect(collect(scaled[None, None], "yl", 0), "x", 1)
    slab = slab.reshape((-1, scaled.shape[1]))
    near_vir, near_occ = slab[:, :n_vir], slab[:, n_vir:]

    vir = both_cores(orbitals_vir, core)
    all_occ = jnp.concatenate([orbitals_occ, lax.ppermute(orbitals_occ, "orb", SWAP)], axis=0)
    occ = both_cores(all_occ, core)

    send_vir = lax.dynamic_slice_in_dim(vir, (1 - part) * half, half, 1)
    keep_vir = lax.dynamic_slice_in_dim(vir, part * half, half, 1)
    away = jnp.dot(near_vir, send_vir, preferred_element_type=f32).astype(bf16)
    arrived = lax.ppermute(away, "orb", SWAP)
    green_vir = jnp.dot(near_vir, keep_vir, preferred_element_type=f32) + arrived.astype(f32)
    keep_screen = lax.dynamic_slice_in_dim(screen, part * half, half, 1)
    keep_occ = lax.dynamic_slice_in_dim(occ, part * half, half, 1)
    occ_side = (green_vir * keep_screen.astype(f32)).astype(bf16)

    green_occ = jnp.dot(near_occ, occ, preferred_element_type=f32)
    vir_side = (green_occ * screen.astype(f32)).astype(bf16)

    dims = (((1,), (1,)), ((), ()))
    occ_term = lax.dot_general(occ_side, keep_occ, dims, preferred_element_type=f32)
    vir_term = lax.dot_general(vir_side, vir, dims, preferred_element_type=f32)
    terms = jnp.concatenate([vir_term.astype(bf16), occ_term.astype(bf16)], axis=1)

    planes = lax.axis_size(("yl", "x"))
    terms = terms.reshape((planes, -1, terms.shape[1]))
    terms = lax.all_to_all(terms, ("yl", "x"), 0, 0, tiled=True)
    terms = jnp.sum(terms.astype(f32), axis=0).astype(bf16)
    owners = lax.axis_size(("z", "orb"))
    terms = terms.reshape((owners, -1, terms.shape[1]))
    terms = lax.all_to_all(terms, ("z", "orb"), 0, 0, tiled=True)
    terms = terms.reshape((owners // 2, 2) + terms.shape[1:]).astype(f32)
    total = jnp.sum(terms, axis=0)
    vir_total = jnp.concatenate([total[0, :, :n_vir], total[1, :, :n_vir]], axis=1)
    occ_first, occ_second = total[0, :, n_vir:], total[1, :, n_vir:]
    occ_total = occ_first + jnp.concatenate(
        [occ_second[:, n_occ:], occ_second[:, :n_occ]], axis=1
    )
    return occ_total.astype(bf16), vir_total.astype(bf16)


def solution(mesh):
    chips = Mesh(mesh.devices.reshape(2, 4, 8, 2, 2), ("yl", "x", "z", "core", "orb"))
    col = ("yl", "x", "z", "core")
    return jax.shard_map(
        local,
        mesh=chips,
        in_specs=(
            P(col, "orb"),
            P(col, "orb"),
            P("orb", col),
            P("orb", col),
            P("orb"),
            P("orb"),
            P(col, None),
        ),
        out_specs=(P(col + ("orb",), None), P(col + ("orb",), None)),
        check_vma=False,
    )
```

```python
import jax
import jax.numpy as jnp
from jax import lax
from jax.sharding import Mesh, PartitionSpec as P

SWAP = ((0, 1), (1, 0))
CHIPS = ("yl", "x", "z")
DIMS = (((1,), (1,)), ((), ()))


def spread(block, axes):
    count = lax.axis_size(axes)
    copies = jnp.broadcast_to(block[None], (count,) + block.shape)
    arrived = lax.all_to_all(copies, axes, 0, 0, tiled=True)
    return arrived.reshape((count * block.shape[0],) + block.shape[1:])


def both_cores(own, core):
    other = lax.ppermute(own, "core", SWAP)
    first = jnp.where(core == 0, own, other)
    second = jnp.where(core == 0, other, own)
    return jnp.concatenate([first, second], axis=1)


def add_up(terms, axes):
    count = lax.axis_size(axes)
    blocks = terms.reshape((count, -1, terms.shape[1]))
    return jnp.sum(lax.all_to_all(blocks, axes, 0, 0, tiled=True).astype(jnp.float32), axis=0)


def local(slab_occ, slab_vir, orbitals_occ, orbitals_vir, occ_energy, vir_energy, screened):
    f32, bf16 = jnp.float32, jnp.bfloat16
    core, part = lax.axis_index("core"), lax.axis_index("orb")
    rows = slab_occ.shape[0] // 2
    n_occ, n_vir = orbitals_occ.shape[0], orbitals_vir.shape[0]

    far_occ = lax.ppermute(orbitals_occ, "orb", SWAP)
    far_vir = lax.ppermute(orbitals_vir, "orb", SWAP)
    occ_mine = both_cores(orbitals_occ, core)
    vir_mine = both_cores(orbitals_vir, core)
    occ_other = both_cores(far_occ, core)
    vir_other = both_cores(far_vir, core)

    scaled = jnp.concatenate(
        [
            (slab_vir.astype(f32) * jnp.exp(-vir_energy)[None, :]).astype(bf16),
            (slab_occ.astype(f32) * jnp.exp(occ_energy)[None, :]).astype(bf16),
        ],
        axis=1,
    )
    keep = lax.dynamic_slice_in_dim(scaled, part * rows, rows, 0)
    away = lax.dynamic_slice_in_dim(scaled, (1 - part) * rows, rows, 0)
    near = jnp.concatenate([keep, lax.ppermute(away, "orb", SWAP)], axis=1)
    slab = spread(spread(near, "z"), ("yl", "x"))
    edges = [n_vir, n_vir + n_occ, 2 * n_vir + n_occ]
    near_vir_mine, near_occ_mine, near_vir_other, near_occ_other = jnp.split(slab, edges, axis=1)

    half = lax.dynamic_slice_in_dim(screened, part * rows, rows, 0)
    screen = lax.all_to_all(half, CHIPS, split_axis=1, concat_axis=0, tiled=True).astype(f32)

    def dot(a, b):
        return jnp.dot(a, b, preferred_element_type=f32)

    def project(a, b):
        return lax.dot_general(a, b, DIMS, preferred_element_type=f32).astype(bf16)

    green_occ = dot(near_occ_mine, occ_mine) + dot(near_occ_other, occ_other)
    vir_side = (green_occ * screen).astype(bf16)
    green_mine = lax.optimization_barrier(dot(near_vir_mine, vir_mine))
    green_vir = green_mine + dot(near_vir_other, vir_other)
    occ_side = (green_vir * screen).astype(bf16)
    terms = jnp.concatenate(
        [
            project(vir_side, vir_mine),
            project(occ_side, occ_mine),
            project(vir_side, vir_other),
            project(occ_side, occ_other),
        ],
        axis=1,
    )

    total = add_up(add_up(terms, ("yl", "x")).astype(bf16), "z").astype(bf16)
    vir_a, occ_a, vir_b, occ_b = jnp.split(total, edges, axis=1)

    def ordered(a, b):
        return jnp.concatenate([jnp.where(part == 0, a, b), jnp.where(part == 0, b, a)], axis=1)

    return ordered(occ_a, occ_b), ordered(vir_a, vir_b)


def solution(mesh):
    chips = Mesh(mesh.devices.reshape(2, 4, 8, 2, 2), ("yl", "x", "z", "core", "orb"))
    col = ("yl", "x", "z", "core")
    return jax.shard_map(
        local,
        mesh=chips,
        in_specs=(
            P(col, "orb"),
            P(col, "orb"),
            P("orb", col),
            P("orb", col),
            P("orb"),
            P("orb"),
            P(col, None),
        ),
        out_specs=(P(col + ("orb",), None), P(col + ("orb",), None)),
        check_vma=False,
    )
```

```python
import jax
import jax.numpy as jnp
from jax import lax
from jax.sharding import Mesh, PartitionSpec as P

SWAP = ((0, 1), (1, 0))
DIMS = (((1,), (1,)), ((), ()))


def spread(block, axes):
    count = lax.axis_size(axes)
    copies = jnp.broadcast_to(block[None], (count,) + block.shape)
    arrived = lax.all_to_all(copies, axes, 0, 0, tiled=True)
    return arrived.reshape((count * block.shape[0],) + block.shape[1:])


def by_place(here, there, place):
    return jnp.concatenate(
        [jnp.where(place == 0, here, there), jnp.where(place == 0, there, here)], axis=0
    )


def both_cores(own, core):
    other = lax.ppermute(own, "core", SWAP)
    first = jnp.where(core == 0, own, other)
    second = jnp.where(core == 0, other, own)
    return jnp.concatenate([first, second], axis=1)


def add_up(terms, axes):
    count = lax.axis_size(axes)
    blocks = terms.reshape((count, -1, terms.shape[1]))
    return jnp.sum(lax.all_to_all(blocks, axes, 0, 0, tiled=True).astype(jnp.float32), axis=0)


def local(slab_occ, slab_vir, orbitals_occ, orbitals_vir, occ_energy, vir_energy, screened):
    f32, bf16 = jnp.float32, jnp.bfloat16
    core, part = lax.axis_index("core"), lax.axis_index("orb")
    rows = slab_occ.shape[0] // 2
    n_occ, n_vir = orbitals_occ.shape[0], orbitals_vir.shape[0]

    level = lax.axis_index("yl")

    scaled = jnp.concatenate(
        [
            (slab_vir.astype(f32) * jnp.exp(-vir_energy)[None, :]).astype(bf16),
            (slab_occ.astype(f32) * jnp.exp(occ_energy)[None, :]).astype(bf16),
        ],
        axis=1,
    )
    keep = lax.dynamic_slice_in_dim(scaled, part * rows, rows, 0)
    away = lax.dynamic_slice_in_dim(scaled, (1 - part) * rows, rows, 0)
    here = jnp.concatenate([keep, lax.ppermute(away, "orb", SWAP)], axis=1)
    across = [(i, 3 - i) for i in range(4)]
    there = jnp.concatenate(
        [lax.ppermute(keep, "yl", SWAP), lax.ppermute(away, ("yl", "orb"), across)], axis=1
    )
    near = by_place(here, there, level)

    half = lax.dynamic_slice_in_dim(screened, part * rows, rows, 0)
    span = half.shape[1] // 2
    here = lax.dynamic_slice_in_dim(half, level * span, span, 1)
    there = lax.dynamic_slice_in_dim(half, (1 - level) * span, span, 1)
    there = lax.ppermute(there, "yl", SWAP)
    screen = by_place(here, there, level)

    occ_mine = both_cores(orbitals_occ, core)
    vir_mine = both_cores(orbitals_vir, core)
    orbitals_occ, orbitals_vir, screen = lax.optimization_barrier(
        (orbitals_occ, orbitals_vir, screen)
    )
    occ_other = both_cores(lax.ppermute(orbitals_occ, "orb", SWAP), core)
    far_vir = lax.ppermute(orbitals_vir, "orb", SWAP)
    cut = n_vir // 32 * 16
    vir_first, vir_last = both_cores(far_vir[:cut], core), both_cores(far_vir[cut:], core)

    slab = spread(spread(near, "z"), "x")
    edges = [n_vir, n_vir + n_occ, n_vir + n_occ + cut, 2 * n_vir + n_occ]
    near_vir, near_occ, near_first, near_last, near_occ_other = jnp.split(slab, edges, axis=1)

    screen = lax.all_to_all(screen, ("x", "z"), split_axis=1, concat_axis=0, tiled=True)
    screen = screen.astype(f32)

    def dot(a, b):
        return jnp.dot(a, b, preferred_element_type=f32)

    def project(a, b):
        return lax.dot_general(a, b, DIMS, preferred_element_type=f32).astype(bf16)

    green_occ = dot(near_occ, occ_mine) + dot(near_occ_other, occ_other)
    vir_side = (green_occ * screen).astype(bf16)
    green_mine = dot(near_vir, vir_mine) + dot(near_first, vir_first)
    green_mine, vir_side = lax.optimization_barrier((green_mine, vir_side))
    early = [project(vir_side, vir_mine), project(vir_side, vir_first)]
    green_vir = green_mine + dot(near_last, vir_last)
    occ_side = (green_vir * screen).astype(bf16)
    terms = jnp.concatenate(
        [
            early[0],
            project(occ_side, occ_mine),
            early[1],
            project(vir_side, vir_last),
            project(occ_side, occ_other),
        ],
        axis=1,
    )

    total = add_up(add_up(terms, "x").astype(bf16), ("z", "yl")).astype(bf16)
    edges = [n_vir, n_vir + n_occ, 2 * n_vir + n_occ]
    vir_a, occ_a, vir_b, occ_b = jnp.split(total, edges, axis=1)

    def ordered(a, b):
        return jnp.concatenate([jnp.where(part == 0, a, b), jnp.where(part == 0, b, a)], axis=1)

    return ordered(occ_a, occ_b), ordered(vir_a, vir_b)


def solution(mesh):
    chips = Mesh(mesh.devices.reshape(2, 4, 8, 2, 2), ("yl", "x", "z", "core", "orb"))
    col = ("yl", "x", "z", "core")
    return jax.shard_map(
        local,
        mesh=chips,
        in_specs=(
            P(col, "orb"),
            P(col, "orb"),
            P("orb", col),
            P("orb", col),
            P("orb"),
            P("orb"),
            P(col, None),
        ),
        out_specs=(P(col + ("orb",), None), P(col + ("orb",), None)),
        check_vma=False,
    )
```

```python
import jax
import jax.numpy as jnp
from jax import lax
from jax.sharding import Mesh, PartitionSpec as P

SWAP = ((0, 1), (1, 0))
CHIPS = ("yl", "x", "z")


def collect(block, axis, dim):
    count, me = lax.axis_size(axis), lax.axis_index(axis)
    shape = block.shape[:dim] + (count,) + block.shape[dim + 1 :]
    held = lax.dynamic_update_slice_in_dim(jnp.zeros(shape, block.dtype), block, me, dim)
    for step in range(1, count):
        piece = lax.ppermute(block, axis, [(i, i ^ step) for i in range(count)])
        held = lax.dynamic_update_slice_in_dim(held, piece, me ^ step, dim)
    return held


def spread(block, axes):
    count = lax.axis_size(axes)
    copies = jnp.broadcast_to(block[None], (count,) + block.shape)
    arrived = lax.all_to_all(copies, axes, 0, 0, tiled=True)
    return arrived.reshape((count * block.shape[0],) + block.shape[1:])


def both_blocks(own, kept):
    other = lax.ppermute(own, "core", SWAP)
    return jnp.where(kept, own, other), jnp.where(kept, other, own)


def local(slab_occ, slab_vir, orbitals_occ, orbitals_vir, occ_energy, vir_energy, screened):
    f32, bf16 = jnp.float32, jnp.bfloat16
    core, part = lax.axis_index("core"), lax.axis_index("orb")
    half = orbitals_occ.shape[1]
    n_occ, n_vir = orbitals_occ.shape[0], orbitals_vir.shape[0]

    raw = spread(jnp.concatenate([slab_vir, slab_occ], axis=1), "z")
    raw, screened = lax.optimization_barrier((raw, screened))

    blocks = screened.reshape((screened.shape[0], -1, 2, half))

    def block_of_screen(index):
        block = lax.dynamic_index_in_dim(blocks, index, 2, keepdims=False)
        return block.reshape((screened.shape[0], -1))

    far_w, keep_w = block_of_screen(1 - part), block_of_screen(part)
    far_w = lax.all_to_all(far_w, CHIPS, split_axis=1, concat_axis=0, tiled=True)
    far_w, keep_w = lax.optimization_barrier((far_w, keep_w))
    keep_w = lax.all_to_all(keep_w, CHIPS, split_axis=1, concat_axis=0, tiled=True)

    scaled_vir = (raw[:, :n_vir].astype(f32) * jnp.exp(-vir_energy)[None, :]).astype(bf16)
    scaled_occ = (raw[:, n_vir:].astype(f32) * jnp.exp(occ_energy)[None, :]).astype(bf16)
    scaled = jnp.concatenate(
        [scaled_vir, scaled_occ, lax.ppermute(scaled_occ, "orb", SWAP)], axis=1
    )
    slab = collect(collect(scaled[None, None], "yl", 0), "x", 1)
    slab = slab.reshape((-1, scaled.shape[1]))
    near_vir, near_occ = slab[:, :n_vir], slab[:, n_vir:]

    kept = core == part
    keep_vir, far_vir = both_blocks(orbitals_vir, kept)
    all_occ = jnp.concatenate([orbitals_occ, lax.ppermute(orbitals_occ, "orb", SWAP)], axis=0)
    keep_occ, far_occ = both_blocks(all_occ, kept)

    def dot(a, b):
        return jnp.dot(a, b, preferred_element_type=f32)

    def project(a, b):
        dims = (((1,), (1,)), ((), ()))
        return lax.dot_general(a, b, dims, preferred_element_type=f32)

    away = dot(near_vir, far_vir).astype(bf16)
    arrived = lax.ppermute(away, "orb", SWAP)
    near_vir, away = lax.optimization_barrier((near_vir, away))
    green_vir = lax.optimization_barrier(dot(near_vir, keep_vir))
    far_side = (dot(near_occ, far_occ) * far_w.astype(f32)).astype(bf16)
    far_term = lax.optimization_barrier(project(far_side, far_vir))

    keep_w = keep_w.astype(f32)
    vir_side = (dot(near_occ, keep_occ) * keep_w).astype(bf16)
    occ_side = ((green_vir + arrived.astype(f32)) * keep_w).astype(bf16)
    vir_term = far_term + project(vir_side, keep_vir)
    occ_term = project(occ_side, keep_occ)
    terms = jnp.concatenate([vir_term.astype(bf16), occ_term.astype(bf16)], axis=1)

    planes = lax.axis_size(("yl", "x"))
    terms = terms.reshape((planes, -1, terms.shape[1]))
    terms = lax.all_to_all(terms, ("yl", "x"), 0, 0, tiled=True)
    terms = jnp.sum(terms.astype(f32), axis=0).astype(bf16)
    owners = lax.axis_size(("z", "orb"))
    terms = terms.reshape((owners, -1, terms.shape[1]))
    terms = lax.all_to_all(terms, ("z", "orb"), 0, 0, tiled=True)
    terms = terms.reshape((owners // 2, 2) + terms.shape[1:]).astype(f32)
    total = jnp.sum(terms, axis=0)
    vir_total = jnp.concatenate([total[0, :, :n_vir], total[1, :, :n_vir]], axis=1)
    occ_first, occ_second = total[0, :, n_vir:], total[1, :, n_vir:]
    occ_total = occ_first + jnp.concatenate(
        [occ_second[:, n_occ:], occ_second[:, :n_occ]], axis=1
    )
    return occ_total.astype(bf16), vir_total.astype(bf16)


def solution(mesh):
    chips = Mesh(mesh.devices.reshape(2, 4, 8, 2, 2), ("yl", "x", "z", "core", "orb"))
    col = ("yl", "x", "z", "core")
    return jax.shard_map(
        local,
        mesh=chips,
        in_specs=(
            P(col, "orb"),
            P(col, "orb"),
            P("orb", col),
            P("orb", col),
            P("orb"),
            P("orb"),
            P(col, None),
        ),
        out_specs=(P(col + ("orb",), None), P(col + ("orb",), None)),
        check_vma=False,
    )
```

```python
import functools

import jax
import jax.numpy as jnp
from jax import lax
from jax.experimental import pallas as pl
from jax.experimental.pallas import tpu as pltpu
from jax.sharding import Mesh, PartitionSpec as P

SWAP = ((0, 1), (1, 0))
CHIPS = ("yl", "x", "z")


def collect(block, axis, dim):
    count, me = lax.axis_size(axis), lax.axis_index(axis)
    shape = block.shape[:dim] + (count,) + block.shape[dim + 1 :]
    held = lax.dynamic_update_slice_in_dim(jnp.zeros(shape, block.dtype), block, me, dim)
    for step in range(1, count):
        piece = lax.ppermute(block, axis, [(i, i ^ step) for i in range(count)])
        held = lax.dynamic_update_slice_in_dim(held, piece, me ^ step, dim)
    return held


def spread(block, axes):
    count = lax.axis_size(axes)
    copies = jnp.broadcast_to(block[None], (count,) + block.shape)
    arrived = lax.all_to_all(copies, axes, 0, 0, tiled=True)
    return arrived.reshape((count * block.shape[0],) + block.shape[1:])


def both_cores(own, core):
    other = lax.ppermute(own, "core", SWAP)
    first = jnp.where(core == 0, own, other)
    second = jnp.where(core == 0, other, own)
    return jnp.concatenate([first, second], axis=1)


def project_kernel(steps, part, near, occ, vir, screen, own, arrived, out, vir_sum, occ_sum):
    f32, bf16 = jnp.float32, jnp.bfloat16
    step = pl.program_id(0)
    dims = (((1,), (1,)), ((), ()))
    weight = screen[...].astype(f32)
    occ_tile = occ[...]
    green = jnp.dot(near[...], occ_tile, preferred_element_type=f32)
    side = (green * weight).astype(bf16)
    term = lax.dot_general(side, vir[...], dims, preferred_element_type=f32)

    @pl.when(step == 0)
    def _():
        vir_sum[...] = term

    @pl.when(step > 0)
    def _():
        vir_sum[...] += term

    @pl.when(step >= steps // 2)
    def _():
        green = own[...] + arrived[...].astype(f32)
        side = (green * weight).astype(bf16)
        term = lax.dot_general(side, occ_tile, dims, preferred_element_type=f32)

        @pl.when(step == steps // 2)
        def _():
            occ_sum[...] = term

        @pl.when(step > steps // 2)
        def _():
            occ_sum[...] += term

    @pl.when(step == steps - 1)
    def _():
        n_vir = vir_sum.shape[1]
        out[:, :n_vir] = vir_sum[...].astype(bf16)
        out[:, n_vir:] = occ_sum[...].astype(bf16)


def project(part, near, occ, vir, screen, own, arrived):
    rows, columns = screen.shape
    steps = 4
    tile = columns // steps
    n_occ, n_vir = occ.shape[0], vir.shape[0]

    def place(step, part):
        block = jnp.where(step < steps // 2, 1 - part[0], part[0])
        return 0, block * (steps // 2) + step % (steps // 2)

    def late(step, part):
        return 0, jnp.maximum(step - steps // 2, 0)

    return pl.pallas_call(
        functools.partial(project_kernel, steps),
        grid_spec=pltpu.PrefetchScalarGridSpec(
            num_scalar_prefetch=1,
            grid=(steps,),
            in_specs=[
                pl.BlockSpec((rows, n_occ), lambda step, part: (0, 0)),
                pl.BlockSpec((n_occ, tile), place),
                pl.BlockSpec((n_vir, tile), place),
                pl.BlockSpec((rows, tile), place),
                pl.BlockSpec((rows, tile), late),
                pl.BlockSpec((rows, tile), late),
            ],
            out_specs=pl.BlockSpec((rows, n_occ + n_vir), lambda step, part: (0, 0)),
            scratch_shapes=[
                pltpu.VMEM((rows, n_vir), jnp.float32),
                pltpu.VMEM((rows, n_occ), jnp.float32),
            ],
        ),
        out_shape=jax.ShapeDtypeStruct((rows, n_occ + n_vir), jnp.bfloat16),
        compiler_params=pltpu.CompilerParams(vmem_limit_bytes=44 * 2**20),
        cost_estimate=pl.CostEstimate(
            flops=2 * rows * columns * (n_vir + n_occ + n_occ // 2),
            bytes_accessed=2 * columns * (n_vir + n_occ + 3 * rows),
            transcendentals=0,
        ),
    )(part[None], near, occ, vir, screen, own, arrived)


def local(slab_occ, slab_vir, orbitals_occ, orbitals_vir, occ_energy, vir_energy, screened):
    f32, bf16 = jnp.float32, jnp.bfloat16
    core, part = lax.axis_index("core"), lax.axis_index("orb")
    half = orbitals_occ.shape[1]
    n_occ, n_vir = orbitals_occ.shape[0], orbitals_vir.shape[0]

    raw = spread(jnp.concatenate([slab_vir, slab_occ], axis=1), "z")
    scaled_vir = (raw[:, :n_vir].astype(f32) * jnp.exp(-vir_energy)[None, :]).astype(bf16)
    scaled_occ = (raw[:, n_vir:].astype(f32) * jnp.exp(occ_energy)[None, :]).astype(bf16)

    mine = jnp.concatenate([scaled_vir, scaled_occ], axis=1)
    mine = collect(mine[None], "x", 0)
    mine, screened = lax.optimization_barrier((mine, screened))

    mine_occ = mine[:, :, n_vir:]
    across = [(i, 3 - i) for i in range(4)]
    there = jnp.concatenate(
        [lax.ppermute(mine, "yl", SWAP), lax.ppermute(mine_occ, ("yl", "orb"), across)], axis=2
    )
    here = jnp.concatenate([mine, lax.ppermute(mine_occ, "orb", SWAP)], axis=2)
    low = lax.axis_index("yl") == 0
    slab = jnp.concatenate([jnp.where(low, here, there), jnp.where(low, there, here)])
    slab = slab.reshape((-1, slab.shape[2]))

    screen = lax.all_to_all(screened, CHIPS, split_axis=1, concat_axis=0, tiled=True)

    near_vir, near_occ = slab[:, :n_vir], slab[:, n_vir:]

    vir = both_cores(orbitals_vir, core)
    all_occ = jnp.concatenate([orbitals_occ, lax.ppermute(orbitals_occ, "orb", SWAP)], axis=0)
    occ = both_cores(all_occ, core)

    send_vir = lax.dynamic_slice_in_dim(vir, (1 - part) * half, half, 1)
    keep_vir = lax.dynamic_slice_in_dim(vir, part * half, half, 1)
    away = jnp.dot(near_vir, send_vir, preferred_element_type=f32).astype(bf16)
    arrived = lax.ppermute(away, "orb", SWAP)
    near_vir, away = lax.optimization_barrier((near_vir, away))
    green_vir = jnp.dot(near_vir, keep_vir, preferred_element_type=f32)
    terms = project(part, near_occ, occ, vir, screen, green_vir, arrived)

    planes = lax.axis_size(("yl", "x"))
    terms = terms.reshape((planes, -1, terms.shape[1]))
    terms = lax.all_to_all(terms, ("yl", "x"), 0, 0, tiled=True)
    terms = jnp.sum(terms.astype(f32), axis=0).astype(bf16)
    owners = lax.axis_size(("z", "orb"))
    terms = terms.reshape((owners, -1, terms.shape[1]))
    terms = lax.all_to_all(terms, ("z", "orb"), 0, 0, tiled=True)
    terms = terms.reshape((owners // 2, 2) + terms.shape[1:]).astype(f32)
    total = jnp.sum(terms, axis=0)
    vir_total = jnp.concatenate([total[0, :, :n_vir], total[1, :, :n_vir]], axis=1)
    occ_first, occ_second = total[0, :, n_vir:], total[1, :, n_vir:]
    occ_total = occ_first + jnp.concatenate(
        [occ_second[:, n_occ:], occ_second[:, :n_occ]], axis=1
    )
    return occ_total.astype(bf16), vir_total.astype(bf16)


def solution(mesh):
    chips = Mesh(mesh.devices.reshape(2, 4, 8, 2, 2), ("yl", "x", "z", "core", "orb"))
    col = ("yl", "x", "z", "core")
    return jax.shard_map(
        local,
        mesh=chips,
        in_specs=(
            P(col, "orb"),
            P(col, "orb"),
            P("orb", col),
            P("orb", col),
            P("orb"),
            P("orb"),
            P(col, None),
        ),
        out_specs=(P(col + ("orb",), None), P(col + ("orb",), None)),
        check_vma=False,
    )
```

```python
import jax
import jax.numpy as jnp
from jax import lax
from jax.experimental import pallas as pl
from jax.experimental.pallas import tpu as pltpu
from jax.sharding import Mesh, PartitionSpec as P

SWAP = ((0, 1), (1, 0))
DIMS = (((1,), (1,)), ((), ()))
CHIPS = ("yl", "x", "z")


def spread(block, axes):
    count = lax.axis_size(axes)
    copies = jnp.broadcast_to(block[None], (count,) + block.shape)
    arrived = lax.all_to_all(copies, axes, 0, 0, tiled=True)
    return arrived.reshape((count * block.shape[0],) + block.shape[1:])


def both_cores(own, core):
    other = lax.ppermute(own, "core", SWAP)
    first = jnp.where(core == 0, own, other)
    second = jnp.where(core == 0, other, own)
    return jnp.concatenate([first, second], axis=1)


def vir_kernel(near, occ, vir, screen, out, total):
    step = pl.program_id(0)
    green = jnp.dot(near[...], occ[...], preferred_element_type=jnp.float32)
    side = (green * screen[...].astype(jnp.float32)).astype(jnp.bfloat16)
    term = lax.dot_general(side, vir[...], DIMS, preferred_element_type=jnp.float32)

    @pl.when(step == 0)
    def _():
        total[...] = term

    @pl.when(step > 0)
    def _():
        total[...] += term

    @pl.when(step == pl.num_programs(0) - 1)
    def _():
        out[...] = total[...].astype(jnp.bfloat16)


def vir_terms(near, occ, vir, screen):
    rows, columns = screen.shape
    tile = columns // 4
    n_occ, n_vir = occ.shape[0], vir.shape[0]
    return pl.pallas_call(
        vir_kernel,
        grid=(4,),
        in_specs=[
            pl.BlockSpec((rows, n_occ), lambda step: (0, 0)),
            pl.BlockSpec((n_occ, tile), lambda step: (0, step)),
            pl.BlockSpec((n_vir, tile), lambda step: (0, step)),
            pl.BlockSpec((rows, tile), lambda step: (0, step)),
        ],
        out_specs=pl.BlockSpec((rows, n_vir), lambda step: (0, 0)),
        out_shape=jax.ShapeDtypeStruct((rows, n_vir), jnp.bfloat16),
        scratch_shapes=[pltpu.VMEM((rows, n_vir), jnp.float32)],
        compiler_params=pltpu.CompilerParams(vmem_limit_bytes=60 * 2**20),
        cost_estimate=pl.CostEstimate(
            flops=2 * rows * columns * (n_vir + n_occ),
            bytes_accessed=2 * columns * (n_vir + n_occ + rows) + 2 * rows * (n_vir + n_occ),
            transcendentals=0,
        ),
    )(near, occ, vir, screen)


def occ_kernel(part, vir_part, occ, screen, own, arrived, out, total):
    step = pl.program_id(0)
    green = own[...] + arrived[...].astype(jnp.float32)
    side = (green * screen[...].astype(jnp.float32)).astype(jnp.bfloat16)
    term = lax.dot_general(side, occ[...], DIMS, preferred_element_type=jnp.float32)

    @pl.when(step == 0)
    def _():
        total[...] = term
        out[:, : vir_part.shape[1]] = vir_part[...]

    @pl.when(step > 0)
    def _():
        out[:, vir_part.shape[1] :] = (total[...] + term).astype(jnp.bfloat16)


def all_terms(part, vir_part, occ, screen, own, arrived):
    rows, kept = own.shape
    tile = kept // 2
    n_occ, n_vir = occ.shape[0], vir_part.shape[1]

    def place(step, part):
        return 0, 2 * part[0] + step

    return pl.pallas_call(
        occ_kernel,
        grid_spec=pltpu.PrefetchScalarGridSpec(
            num_scalar_prefetch=1,
            grid=(2,),
            in_specs=[
                pl.BlockSpec((rows, n_vir), lambda step, part: (0, 0)),
                pl.BlockSpec((n_occ, tile), place),
                pl.BlockSpec((rows, tile), place),
                pl.BlockSpec((rows, tile), lambda step, part: (0, step)),
                pl.BlockSpec((rows, tile), lambda step, part: (0, step)),
            ],
            out_specs=pl.BlockSpec((rows, n_vir + n_occ), lambda step, part: (0, 0)),
            scratch_shapes=[pltpu.VMEM((rows, n_occ), jnp.float32)],
        ),
        out_shape=jax.ShapeDtypeStruct((rows, n_vir + n_occ), jnp.bfloat16),
        compiler_params=pltpu.CompilerParams(vmem_limit_bytes=60 * 2**20),
        cost_estimate=pl.CostEstimate(
            flops=2 * rows * kept * n_occ,
            bytes_accessed=kept * (2 * n_occ + 8 * rows) + 4 * rows * n_vir,
            transcendentals=0,
        ),
    )(part[None], vir_part, occ, screen, own, arrived)


def local(slab_occ, slab_vir, orbitals_occ, orbitals_vir, occ_energy, vir_energy, screened):
    f32, bf16 = jnp.float32, jnp.bfloat16
    core, part = lax.axis_index("core"), lax.axis_index("orb")
    half = orbitals_occ.shape[1]
    n_occ, n_vir = orbitals_occ.shape[0], orbitals_vir.shape[0]

    raw = spread(jnp.concatenate([slab_vir, slab_occ], axis=1), ("x", "z"))
    raw, screened = lax.optimization_barrier((raw, screened))
    raw = raw.reshape((lax.axis_size("x"), -1, raw.shape[1]))
    mine_vir = (raw[:, :, :n_vir].astype(f32) * jnp.exp(-vir_energy)).astype(bf16)
    mine_occ = (raw[:, :, n_vir:].astype(f32) * jnp.exp(occ_energy)).astype(bf16)

    low = lax.axis_index("yl") == 0

    def rows_in_order(here, there):
        pair = jnp.concatenate([jnp.where(low, here, there), jnp.where(low, there, here)])
        return pair.reshape((-1, pair.shape[2]))

    far_rows = lax.ppermute(mine_vir, "yl", SWAP)
    across = [(i, 3 - i) for i in range(4)]
    there = [lax.ppermute(mine_occ, "yl", SWAP), lax.ppermute(mine_occ, ("yl", "orb"), across)]
    here = [mine_occ, lax.ppermute(mine_occ, "orb", SWAP)]
    near_occ = rows_in_order(jnp.concatenate(here, axis=2), jnp.concatenate(there, axis=2))

    screen = lax.all_to_all(screened, CHIPS, split_axis=1, concat_axis=0, tiled=True)


    vir = both_cores(orbitals_vir, core)
    all_occ = jnp.concatenate([orbitals_occ, lax.ppermute(orbitals_occ, "orb", SWAP)], axis=0)
    occ = both_cores(all_occ, core)

    send_vir = lax.dynamic_slice_in_dim(vir, (1 - part) * half, half, 1)
    keep_vir = lax.dynamic_slice_in_dim(vir, part * half, half, 1)

    def partner_part(near):
        away = jnp.dot(near.reshape((-1, n_vir)), send_vir, preferred_element_type=f32)
        away = away.astype(bf16).reshape(near.shape[:2] + (half,))
        return away, lax.ppermute(away, "orb", SWAP)

    away, here = partner_part(mine_vir)
    away, there = partner_part(far_rows)
    arrived = rows_in_order(here, there)
    near_vir, away = lax.optimization_barrier((rows_in_order(mine_vir, far_rows), away))
    green_vir = jnp.dot(near_vir, keep_vir, preferred_element_type=f32)
    vir_part = vir_terms(near_occ, occ, vir, screen)
    terms = all_terms(part, vir_part, occ, screen, green_vir, arrived)

    planes = lax.axis_size(("yl", "x"))
    terms = terms.reshape((planes, -1, terms.shape[1]))
    terms = lax.all_to_all(terms, ("yl", "x"), 0, 0, tiled=True)
    terms = jnp.sum(terms.astype(f32), axis=0).astype(bf16)
    owners = lax.axis_size(("z", "orb"))
    terms = terms.reshape((owners, -1, terms.shape[1]))
    terms = lax.all_to_all(terms, ("z", "orb"), 0, 0, tiled=True)
    terms = terms.reshape((owners // 2, 2) + terms.shape[1:]).astype(f32)
    total = jnp.sum(terms, axis=0)
    vir_total = jnp.concatenate([total[0, :, :n_vir], total[1, :, :n_vir]], axis=1)
    occ_first, occ_second = total[0, :, n_vir:], total[1, :, n_vir:]
    occ_total = occ_first + jnp.concatenate(
        [occ_second[:, n_occ:], occ_second[:, :n_occ]], axis=1
    )
    return occ_total.astype(bf16), vir_total.astype(bf16)


def solution(mesh):
    chips = Mesh(mesh.devices.reshape(2, 4, 8, 2, 2), ("yl", "x", "z", "core", "orb"))
    col = ("yl", "x", "z", "core")
    return jax.shard_map(
        local,
        mesh=chips,
        in_specs=(
            P(col, "orb"),
            P(col, "orb"),
            P("orb", col),
            P("orb", col),
            P("orb"),
            P("orb"),
            P(col, None),
        ),
        out_specs=(P(col + ("orb",), None), P(col + ("orb",), None)),
        check_vma=False,
    )
```

```python
import jax
import jax.numpy as jnp
from jax import lax
from jax.sharding import Mesh, PartitionSpec as P

SWAP = ((0, 1), (1, 0))
CHIPS = ("yl", "x", "z")


def collect(block, axis, dim):
    count, me = lax.axis_size(axis), lax.axis_index(axis)
    shape = block.shape[:dim] + (count,) + block.shape[dim + 1 :]
    held = lax.dynamic_update_slice_in_dim(jnp.zeros(shape, block.dtype), block, me, dim)
    for step in range(1, count):
        piece = lax.ppermute(block, axis, [(i, i ^ step) for i in range(count)])
        held = lax.dynamic_update_slice_in_dim(held, piece, me ^ step, dim)
    return held


def spread(block, axes):
    count = lax.axis_size(axes)
    copies = jnp.broadcast_to(block[None], (count,) + block.shape)
    arrived = lax.all_to_all(copies, axes, 0, 0, tiled=True)
    return arrived.reshape((count * block.shape[0],) + block.shape[1:])


def both_cores(own, core):
    other = lax.ppermute(own, "core", SWAP)
    first = jnp.where(core == 0, own, other)
    second = jnp.where(core == 0, other, own)
    return jnp.concatenate([first, second], axis=1)


def local(slab_occ, slab_vir, orbitals_occ, orbitals_vir, occ_energy, vir_energy, screened):
    f32, bf16 = jnp.float32, jnp.bfloat16
    core, part = lax.axis_index("core"), lax.axis_index("orb")
    half = orbitals_occ.shape[1]
    n_occ, n_vir = orbitals_occ.shape[0], orbitals_vir.shape[0]

    raw = spread(jnp.concatenate([slab_vir, slab_occ], axis=1), "z")
    raw, screened = lax.optimization_barrier((raw, screened))

    screen = lax.all_to_all(screened, CHIPS, split_axis=1, concat_axis=0, tiled=True)

    scaled_vir = (raw[:, :n_vir].astype(f32) * jnp.exp(-vir_energy)[None, :]).astype(bf16)
    scaled_occ = (raw[:, n_vir:].astype(f32) * jnp.exp(occ_energy)[None, :]).astype(bf16)
    scaled = jnp.concatenate(
        [scaled_vir, scaled_occ, lax.ppermute(scaled_occ, "orb", SWAP)], axis=1
    )
    slab = collect(collect(scaled[None, None], "yl", 0), "x", 1)
    slab = slab.reshape((-1, scaled.shape[1]))
    near_vir, near_occ = slab[:, :n_vir], slab[:, n_vir:]

    vir = both_cores(orbitals_vir, core)
    all_occ = jnp.concatenate([orbitals_occ, lax.ppermute(orbitals_occ, "orb", SWAP)], axis=0)
    occ = both_cores(all_occ, core)

    send_vir = lax.dynamic_slice_in_dim(vir, (1 - part) * half, half, 1)
    keep_vir = lax.dynamic_slice_in_dim(vir, part * half, half, 1)
    away = jnp.dot(near_vir, send_vir, preferred_element_type=f32).astype(bf16)
    arrived = lax.ppermute(away, "orb", SWAP)
    near_vir, away = lax.optimization_barrier((near_vir, away))
    own = lax.optimization_barrier(jnp.dot(near_vir, keep_vir, preferred_element_type=f32))

    dims = (((1,), (1,)), ((), ()))
    green_occ = jnp.dot(near_occ, occ, preferred_element_type=f32)
    vir_side = (green_occ * screen.astype(f32)).astype(bf16)
    vir_term = lax.dot_general(vir_side, vir, dims, preferred_element_type=f32).astype(bf16)

    def exchange(terms):
        blocks = terms.reshape((lax.axis_size(("yl", "x")), -1, terms.shape[1]))
        return lax.all_to_all(blocks, ("yl", "x"), 0, 0, tiled=True)

    def add_up(blocks):
        return jnp.sum(blocks.astype(f32), axis=0).astype(bf16)

    vir_blocks = exchange(vir_term)

    green_vir = own + arrived.astype(f32)
    keep_screen = lax.dynamic_slice_in_dim(screen, part * half, half, 1)
    keep_occ = lax.dynamic_slice_in_dim(occ, part * half, half, 1)
    occ_side = (green_vir * keep_screen.astype(f32)).astype(bf16)
    occ_term = lax.dot_general(occ_side, keep_occ, dims, preferred_element_type=f32).astype(bf16)
    occ_term, vir_blocks = lax.optimization_barrier((occ_term, vir_blocks))
    terms = jnp.concatenate([add_up(vir_blocks), add_up(exchange(occ_term))], axis=1)

    owners = lax.axis_size(("z", "orb"))
    terms = terms.reshape((owners, -1, terms.shape[1]))
    terms = lax.all_to_all(terms, ("z", "orb"), 0, 0, tiled=True)
    terms = terms.reshape((owners // 2, 2) + terms.shape[1:]).astype(f32)
    total = jnp.sum(terms, axis=0)
    vir_total = jnp.concatenate([total[0, :, :n_vir], total[1, :, :n_vir]], axis=1)
    occ_first, occ_second = total[0, :, n_vir:], total[1, :, n_vir:]
    occ_total = occ_first + jnp.concatenate(
        [occ_second[:, n_occ:], occ_second[:, :n_occ]], axis=1
    )
    return occ_total.astype(bf16), vir_total.astype(bf16)


def solution(mesh):
    chips = Mesh(mesh.devices.reshape(2, 4, 8, 2, 2), ("yl", "x", "z", "core", "orb"))
    col = ("yl", "x", "z", "core")
    return jax.shard_map(
        local,
        mesh=chips,
        in_specs=(
            P(col, "orb"),
            P(col, "orb"),
            P("orb", col),
            P("orb", col),
            P("orb"),
            P("orb"),
            P(col, None),
        ),
        out_specs=(P(col + ("orb",), None), P(col + ("orb",), None)),
        check_vma=False,
    )
```

```python
import jax
import jax.numpy as jnp
from jax import lax
from jax.sharding import Mesh, PartitionSpec as P

SWAP = ((0, 1), (1, 0))
CHIPS = ("yl", "x", "z")


def pieces_along(block, axis):
    count, me = lax.axis_size(axis), lax.axis_index(axis)
    pieces = [(block, me)]
    for step in range(1, count):
        pairs = [(i, i ^ step) for i in range(count)]
        pieces.append((lax.ppermute(block, axis, pairs), me ^ step))
    return pieces


def in_order(pieces, dim):
    first = pieces[0][0]
    held = jnp.zeros(first.shape[:dim] + (len(pieces),) + first.shape[dim:], first.dtype)
    for piece, place in pieces:
        held = lax.dynamic_update_index_in_dim(held, piece, place, dim)
    return held.reshape((-1, first.shape[-1]))


def spread(block, axes):
    count = lax.axis_size(axes)
    copies = jnp.broadcast_to(block[None], (count,) + block.shape)
    arrived = lax.all_to_all(copies, axes, 0, 0, tiled=True)
    return arrived.reshape((count * block.shape[0],) + block.shape[1:])


def both_cores(own, core):
    other = lax.ppermute(own, "core", SWAP)
    first = jnp.where(core == 0, own, other)
    second = jnp.where(core == 0, other, own)
    return jnp.concatenate([first, second], axis=1)


def local(slab_occ, slab_vir, orbitals_occ, orbitals_vir, occ_energy, vir_energy, screened):
    f32, bf16 = jnp.float32, jnp.bfloat16
    core, part = lax.axis_index("core"), lax.axis_index("orb")
    half = orbitals_occ.shape[1]
    n_occ, n_vir = orbitals_occ.shape[0], orbitals_vir.shape[0]

    raw = spread(jnp.concatenate([slab_vir, slab_occ], axis=1), "z")
    raw, screened = lax.optimization_barrier((raw, screened))

    screen = lax.all_to_all(screened, CHIPS, split_axis=1, concat_axis=0, tiled=True)

    scaled_vir = (raw[:, :n_vir].astype(f32) * jnp.exp(-vir_energy)[None, :]).astype(bf16)
    scaled_occ = (raw[:, n_vir:].astype(f32) * jnp.exp(occ_energy)[None, :]).astype(bf16)
    scaled = jnp.concatenate(
        [scaled_vir, scaled_occ, lax.ppermute(scaled_occ, "orb", SWAP)], axis=1
    )
    pair = in_order(pieces_along(scaled, "yl"), 0).reshape((2,) + scaled.shape)
    pieces = pieces_along(pair, "x")

    vir = both_cores(orbitals_vir, core)
    all_occ = jnp.concatenate([orbitals_occ, lax.ppermute(orbitals_occ, "orb", SWAP)], axis=0)
    occ = both_cores(all_occ, core)

    send_vir = lax.dynamic_slice_in_dim(vir, (1 - part) * half, half, 1)
    keep_vir = lax.dynamic_slice_in_dim(vir, part * half, half, 1)
    owns, parts = [], []
    for index, (piece, place) in enumerate(pieces):
        if parts:
            piece, parts[-1] = lax.optimization_barrier((piece, parts[-1]))
            pieces[index] = piece, place
        near_vir = piece[:, :, :n_vir].reshape((-1, n_vir))
        away = jnp.dot(near_vir, send_vir, preferred_element_type=f32).astype(bf16)
        parts.append(lax.ppermute(away, "orb", SWAP))
        owns.append(lax.optimization_barrier(jnp.dot(near_vir, keep_vir, preferred_element_type=f32)))
    near_occ = in_order([(piece[:, :, n_vir:], place) for piece, place in pieces], 1)
    dims = (((1,), (1,)), ((), ()))
    green_occ = jnp.dot(near_occ, occ, preferred_element_type=f32)
    vir_side = (green_occ * screen.astype(f32)).astype(bf16)
    vir_term = lax.dot_general(vir_side, vir, dims, preferred_element_type=f32).astype(bf16)
    vir_term, parts[-1] = lax.optimization_barrier((vir_term, parts[-1]))

    greens = [
        ((own + arrived.astype(f32)).reshape(piece.shape[:2] + (half,)), place)
        for own, arrived, (piece, place) in zip(owns, parts, pieces)
    ]
    green_vir = in_order(greens, 1)
    keep_screen = lax.dynamic_slice_in_dim(screen, part * half, half, 1)
    keep_occ = lax.dynamic_slice_in_dim(occ, part * half, half, 1)
    occ_side = (green_vir * keep_screen.astype(f32)).astype(bf16)
    occ_term = lax.dot_general(occ_side, keep_occ, dims, preferred_element_type=f32).astype(bf16)
    terms = jnp.concatenate([vir_term, occ_term], axis=1)

    planes = lax.axis_size(("yl", "x"))
    terms = terms.reshape((planes, -1, terms.shape[1]))
    terms = lax.all_to_all(terms, ("yl", "x"), 0, 0, tiled=True)
    terms = jnp.sum(terms.astype(f32), axis=0).astype(bf16)
    owners = lax.axis_size(("z", "orb"))
    terms = terms.reshape((owners, -1, terms.shape[1]))
    terms = lax.all_to_all(terms, ("z", "orb"), 0, 0, tiled=True)
    terms = terms.reshape((owners // 2, 2) + terms.shape[1:]).astype(f32)
    total = jnp.sum(terms, axis=0)
    vir_total = jnp.concatenate([total[0, :, :n_vir], total[1, :, :n_vir]], axis=1)
    occ_first, occ_second = total[0, :, n_vir:], total[1, :, n_vir:]
    occ_total = occ_first + jnp.concatenate(
        [occ_second[:, n_occ:], occ_second[:, :n_occ]], axis=1
    )
    return occ_total.astype(bf16), vir_total.astype(bf16)


def solution(mesh):
    chips = Mesh(mesh.devices.reshape(2, 4, 8, 2, 2), ("yl", "x", "z", "core", "orb"))
    col = ("yl", "x", "z", "core")
    return jax.shard_map(
        local,
        mesh=chips,
        in_specs=(
            P(col, "orb"),
            P(col, "orb"),
            P("orb", col),
            P("orb", col),
            P("orb"),
            P("orb"),
            P(col, None),
        ),
        out_specs=(P(col + ("orb",), None), P(col + ("orb",), None)),
        check_vma=False,
    )
```

```python
import jax
import jax.numpy as jnp
from jax import lax
from jax.sharding import Mesh, PartitionSpec as P

SWAP = ((0, 1), (1, 0))
CHIPS = ("yl", "x", "z")


def pieces_along(block, axis):
    count, me = lax.axis_size(axis), lax.axis_index(axis)
    pieces = [(block, me)]
    for step in range(1, count):
        pairs = [(i, i ^ step) for i in range(count)]
        pieces.append((lax.ppermute(block, axis, pairs), me ^ step))
    return pieces


def in_order(pieces, dim):
    first = pieces[0][0]
    held = jnp.zeros(first.shape[:dim] + (len(pieces),) + first.shape[dim:], first.dtype)
    for piece, place in pieces:
        held = lax.dynamic_update_index_in_dim(held, piece, place, dim)
    return held.reshape((-1, first.shape[-1]))


def spread(block, axes):
    count = lax.axis_size(axes)
    copies = jnp.broadcast_to(block[None], (count,) + block.shape)
    arrived = lax.all_to_all(copies, axes, 0, 0, tiled=True)
    return arrived.reshape((count * block.shape[0],) + block.shape[1:])


def both_cores(own, core):
    other = lax.ppermute(own, "core", SWAP)
    first = jnp.where(core == 0, own, other)
    second = jnp.where(core == 0, other, own)
    return jnp.concatenate([first, second], axis=1)


def local(slab_occ, slab_vir, orbitals_occ, orbitals_vir, occ_energy, vir_energy, screened):
    f32, bf16 = jnp.float32, jnp.bfloat16
    core, part = lax.axis_index("core"), lax.axis_index("orb")
    half = orbitals_occ.shape[1]
    n_occ, n_vir = orbitals_occ.shape[0], orbitals_vir.shape[0]

    raw = spread(jnp.concatenate([slab_vir, slab_occ], axis=1), "z")
    raw, screened = lax.optimization_barrier((raw, screened))

    screen = lax.all_to_all(screened, CHIPS, split_axis=1, concat_axis=0, tiled=True)

    scaled_vir = (raw[:, :n_vir].astype(f32) * jnp.exp(-vir_energy)[None, :]).astype(bf16)
    scaled_occ = (raw[:, n_vir:].astype(f32) * jnp.exp(occ_energy)[None, :]).astype(bf16)
    scaled = jnp.concatenate(
        [scaled_vir, scaled_occ, lax.ppermute(scaled_occ, "orb", SWAP)], axis=1
    )
    pair = in_order(pieces_along(scaled, "yl"), 0).reshape((2,) + scaled.shape)
    pieces = pieces_along(pair, "x")

    vir = both_cores(orbitals_vir, core)
    all_occ = jnp.concatenate([orbitals_occ, lax.ppermute(orbitals_occ, "orb", SWAP)], axis=0)
    occ = both_cores(all_occ, core)

    send_vir = lax.dynamic_slice_in_dim(vir, (1 - part) * half, half, 1)
    keep_vir = lax.dynamic_slice_in_dim(vir, part * half, half, 1)
    owns, parts, groups = [], [], [(0, 1), (2, 3)]
    for group in groups:
        if parts:
            ready, parts[-1] = lax.optimization_barrier(([pieces[i] for i in group], parts[-1]))
            pieces[group[0] : group[-1] + 1] = ready
        near_vir = jnp.concatenate([pieces[i][0][:, :, :n_vir].reshape((-1, n_vir)) for i in group])
        away = jnp.dot(near_vir, send_vir, preferred_element_type=f32).astype(bf16)
        parts.append(lax.ppermute(away, "orb", SWAP))
        owns.append(lax.optimization_barrier(jnp.dot(near_vir, keep_vir, preferred_element_type=f32)))
    near_occ = in_order([(piece[:, :, n_vir:], place) for piece, place in pieces], 1)
    dims = (((1,), (1,)), ((), ()))
    green_occ = jnp.dot(near_occ, occ, preferred_element_type=f32)
    vir_side = (green_occ * screen.astype(f32)).astype(bf16)
    vir_term = lax.dot_general(vir_side, vir, dims, preferred_element_type=f32).astype(bf16)
    vir_term, parts[-1] = lax.optimization_barrier((vir_term, parts[-1]))

    greens = []
    for group, own, arrived in zip(groups, owns, parts):
        green = (own + arrived.astype(f32)).reshape((len(group), 2, -1, half))
        greens += [(green[j], pieces[i][1]) for j, i in enumerate(group)]
    green_vir = in_order(greens, 1)
    keep_screen = lax.dynamic_slice_in_dim(screen, part * half, half, 1)
    keep_occ = lax.dynamic_slice_in_dim(occ, part * half, half, 1)
    occ_side = (green_vir * keep_screen.astype(f32)).astype(bf16)
    occ_term = lax.dot_general(occ_side, keep_occ, dims, preferred_element_type=f32).astype(bf16)
    terms = jnp.concatenate([vir_term, occ_term], axis=1)

    planes = lax.axis_size(("yl", "x"))
    terms = terms.reshape((planes, -1, terms.shape[1]))
    terms = lax.all_to_all(terms, ("yl", "x"), 0, 0, tiled=True)
    terms = jnp.sum(terms.astype(f32), axis=0).astype(bf16)
    owners = lax.axis_size(("z", "orb"))
    terms = terms.reshape((owners, -1, terms.shape[1]))
    terms = lax.all_to_all(terms, ("z", "orb"), 0, 0, tiled=True)
    terms = terms.reshape((owners // 2, 2) + terms.shape[1:]).astype(f32)
    total = jnp.sum(terms, axis=0)
    vir_total = jnp.concatenate([total[0, :, :n_vir], total[1, :, :n_vir]], axis=1)
    occ_first, occ_second = total[0, :, n_vir:], total[1, :, n_vir:]
    occ_total = occ_first + jnp.concatenate(
        [occ_second[:, n_occ:], occ_second[:, :n_occ]], axis=1
    )
    return occ_total.astype(bf16), vir_total.astype(bf16)


def solution(mesh):
    chips = Mesh(mesh.devices.reshape(2, 4, 8, 2, 2), ("yl", "x", "z", "core", "orb"))
    col = ("yl", "x", "z", "core")
    return jax.shard_map(
        local,
        mesh=chips,
        in_specs=(
            P(col, "orb"),
            P(col, "orb"),
            P("orb", col),
            P("orb", col),
            P("orb"),
            P("orb"),
            P(col, None),
        ),
        out_specs=(P(col + ("orb",), None), P(col + ("orb",), None)),
        check_vma=False,
    )
```
